512 devices in a mesh: replica: 32 (over x, z_lo), fsdp: 16 (over z_hi, y, core).
Axes of the slice: x: 4, y: 4, z: 16 (z_hi: 2, z_lo: 8; z = z_hi * 8 + z_lo), core: 2. Of those that a mesh axis runs over, the one named last changes fastest.
Arguments:
- acts: bfloat16 [65536, 8192], P(('replica', 'fsdp')), may hold values from -6 to 6
- norm_gain: bfloat16 [8192], replicated, may hold values from 0.099609375 to 1.8984375
- key_weight: bfloat16 [32, 8192, 512], P('replica', 'fsdp'), may hold values from -6 to 6
- key_cotangent: bfloat16 [65536, 512], P(('replica', 'fsdp')), may hold values from -6 to 6
- pending_delta: bfloat16 [32, 8192, 128], P('replica', 'fsdp'), may hold values from -6 to 6
- fragment_index: int32 [1], replicated, may hold values from 0 to 384
- global_frag: float32 [8192, 128], P('fsdp'), may hold values from -6 to 6
- outer_mom: float32 [8192, 128], P('fsdp'), may hold values from -3 to 3
Outputs:
- key_out: bfloat16 [65536, 512], P(('replica', 'fsdp'))
- new_weight: bfloat16 [32, 8192, 512], P('replica', 'fsdp')
- global_new: float32 [8192, 128], P('fsdp')
- mom_new: float32 [8192, 128], P('fsdp')
The draws below stay inside these ranges and needn't reach their ends.
All inputs are finite; a program needn't handle non-finite values.
Results may differ from the reference program's by a relative error of at most 0.015.
Values may be sent and summed in bfloat16 or wider, within the bound.
No kernel may reach another device: no remote copies, remote signals or barrier semaphores. Data moves between devices by JAX's collectives and lax.ppermute only.
A program may use at most 64 MiB of HBM per device.

```python
import jax
import jax.numpy as jnp
from jax import lax

D = 8192
HD = 128
KVW = 512
REPLICAS = 32
ROWS = 65536


def block_scale(own_key, dims, shards, low, top_value):
    def one(dim, blocks):
        steps = jax.random.uniform(jax.random.fold_in(jax.random.fold_in(own_key, 6), dim), (blocks,), jnp.float32, low / len(shards), top_value / len(shards))
        return jnp.repeat(jnp.exp(steps), dims[dim] // blocks).reshape((-1,) + (1,) * (len(dims) - dim - 1))

    factor_of = one(*shards[0])
    for cut in shards[1:]:
        factor_of = factor_of * one(*cut)
    return factor_of


def bell_draw(stream_key, shape, deviation, limit, split=(), held_as=jnp.bfloat16):
    array = jax.random.normal(stream_key, shape, jnp.float32) * deviation
    if len(split) > 0:
        array = block_scale(stream_key, shape, split, -0.22, 0.18) * array
    return jnp.clip(array, min=-limit, max=limit).astype(held_as)


def setup_inputs(seed: int = 0) -> dict:
    streams_of = jax.random.split(jax.random.key(seed), 9)
    return {
        "acts": bell_draw(streams_of[0], (ROWS, D), 1.0, 6.0, ((0, 512),)),
        "norm_gain": jnp.clip(1.0 + 0.18 * jax.random.normal(streams_of[1], (D,), jnp.float32), 0.099609375, 1.8984375).astype(jnp.bfloat16),
        "key_weight": bell_draw(streams_of[2], (REPLICAS, D, KVW), 1.0, 6.0, ((0, 32), (1, 16))),
        "key_cotangent": bell_draw(streams_of[3], (ROWS, KVW), 1.0, 6.0, ((0, 512),)),
        "pending_delta": bell_draw(streams_of[4], (REPLICAS, D, HD), 1.0, 6.0, ((0, 32), (1, 16))),
        "fragment_index": jax.random.randint(streams_of[5], (1,), 0, KVW - HD + 1).astype(jnp.int32),
        "global_frag": bell_draw(streams_of[6], (D, HD), 1.0, 6.0, ((0, 16),), jnp.float32),
        "outer_mom": bell_draw(streams_of[7], (D, HD), 0.5, 3.0, ((0, 16),), jnp.float32),
    }


inner_rate = 0.5
outer_rate = 0.7
momentum_coef = 0.9
blend_coef = 0.5

def place_fragment(global_new, start, kv_width):
    placed = jnp.zeros((global_new.shape[0], kv_width), global_new.dtype)
    placed = lax.dynamic_update_slice(placed, global_new, (jnp.zeros((), jnp.int32), start.astype(jnp.int32)))
    column = lax.broadcasted_iota(jnp.int32, (1, kv_width), 1) - start.astype(jnp.int32)
    inside = (column >= 0) & (column < global_new.shape[1])
    return (placed, inside)

def reference(acts, norm_gain, key_weight, key_cotangent, pending_delta, fragment_index, global_frag, outer_mom):
    token_rows = acts.astype(jnp.float32)
    rms_scale = lax.rsqrt(lax.optimization_barrier(jnp.mean(token_rows * token_rows, axis=-1, keepdims=True)) + 1e-05)
    normed = (token_rows * rms_scale * norm_gain.astype(jnp.float32)).astype(jnp.bfloat16)
    inverse_root = D ** (-0.5)
    replicas = key_weight.shape[0]
    per_replica = acts.shape[0] // replicas
    kv_width = key_weight.shape[2]
    mean_delta = lax.optimization_barrier(jnp.sum(pending_delta.astype(jnp.float32), axis=0)) / replicas
    mom_new = momentum_coef * outer_mom + mean_delta
    global_new = global_frag - outer_rate * (momentum_coef * mom_new + mean_delta)
    placed, in_fragment = place_fragment(global_new, fragment_index[0], kv_width)
    normed_split = normed.reshape(replicas, per_replica, normed.shape[1])
    cot_split = key_cotangent.reshape(replicas, per_replica, kv_width)

    def one_replica(items):
        normed_here, weight_here, cot_here = items
        key_here = (jnp.dot(normed_here, weight_here, preferred_element_type=jnp.float32) * inverse_root).astype(jnp.bfloat16)
        gradient = jnp.dot(normed_here.T, cot_here, preferred_element_type=jnp.float32) * inverse_root
        stepped = weight_here.astype(jnp.float32) - inner_rate * gradient
        blended = jnp.where(in_fragment, blend_coef * stepped + (1.0 - blend_coef) * placed, stepped)
        return (key_here, blended.astype(jnp.bfloat16))
    key_out, new_weight = lax.map(one_replica, (normed_split, key_weight, cot_split))
    return (key_out.reshape(acts.shape[0], kv_width), new_weight, global_new, mom_new)
```

```python
import jax
import jax.numpy as jnp
from jax import lax
from jax.experimental import pallas as pl
from jax.experimental.pallas import tpu as pltpu
from jax.sharding import PartitionSpec as P

D = 8192
HALF = 8
PARTS = 16
ROWS_IN = 128
BLOCK = 512
KVW = 512
INV_ROOT = D ** (-0.5)

inner_rate = 0.5
outer_rate = 0.7
momentum_coef = 0.9
blend_coef = 0.5

HALVES = [list(range(0, HALF)), list(range(HALF, PARTS))]
ALONG_X = [[x * 8 + z for x in range(4)] for z in range(8)]
ALONG_Z = [[x * 8 + z for z in range(8)] for x in range(4)]
ACROSS = [(f, f ^ HALF) for f in range(PARTS)]

TOK = 32


def norm_kernel(half_ref, acts_ref, gain_ref, cot_ref, far_ref, near_ref):
    half = half_ref[0]
    rows = acts_ref[...].astype(jnp.float32)
    scale = lax.rsqrt(jnp.mean(rows * rows, axis=-1, keepdims=True) + 1e-05)
    cot = cot_ref[...]
    span = HALF * BLOCK
    for j in range(HALF):
        for which, out in ((half, near_ref), (1 - half, far_ref)):
            at = pl.ds(pl.multiple_of(which * span + j * BLOCK, BLOCK), BLOCK)
            part = acts_ref[:, at].astype(jnp.float32) * scale * gain_ref[:, at].astype(jnp.float32)
            out[j, :, 0:BLOCK] = part.astype(jnp.bfloat16)
        far_ref[j, :, BLOCK : BLOCK + KVW] = cot


def normalise(half, acts, gain, cot):
    return pl.pallas_call(
        norm_kernel,
        grid_spec=pltpu.PrefetchScalarGridSpec(
            num_scalar_prefetch=1,
            grid=(ROWS_IN // TOK,),
            in_specs=[
                pl.BlockSpec((TOK, D), lambda i, h: (i, 0)),
                pl.BlockSpec((1, D), lambda i, h: (0, 0)),
                pl.BlockSpec((TOK, KVW), lambda i, h: (i, 0)),
            ],
            out_specs=[
                pl.BlockSpec((HALF, TOK, BLOCK + KVW), lambda i, h: (0, i, 0)),
                pl.BlockSpec((HALF, TOK, BLOCK), lambda i, h: (0, i, 0)),
            ],
        ),
        out_shape=[
            jax.ShapeDtypeStruct((HALF, ROWS_IN, BLOCK + KVW), jnp.bfloat16),
            jax.ShapeDtypeStruct((HALF, ROWS_IN, BLOCK), jnp.bfloat16),
        ],
        compiler_params=pltpu.CompilerParams(vmem_limit_bytes=32 * 1024 * 1024),
        name="normalise",
    )(half, acts, gain, cot)


def transposed_dot(left, right):
    return lax.dot_general(left, right, (((0,), (0,)), ((), ())), preferred_element_type=jnp.float32)


def far_kernel(normed_ref, cot_ref, out_ref):
    out_ref[...] = (transposed_dot(normed_ref[...], cot_ref[...]) * INV_ROOT).astype(jnp.bfloat16)


def far_gradient(far):
    tokens = far.shape[0]
    step = 256
    return pl.pallas_call(
        far_kernel,
        grid=(BLOCK // step,),
        in_specs=[
            pl.BlockSpec((tokens, step), lambda i: (0, i)),
            pl.BlockSpec((tokens, KVW), lambda i: (0, BLOCK // KVW)),
        ],
        out_specs=pl.BlockSpec((step, KVW), lambda i: (i, 0)),
        out_shape=jax.ShapeDtypeStruct((BLOCK, KVW), jnp.bfloat16),
        compiler_params=pltpu.CompilerParams(vmem_limit_bytes=32 * 1024 * 1024),
        name="far_gradient",
    )(far, far)


def near_kernel(far_ref, near_ref, near_weight_ref, far_weight_ref, keys_ref, stepped_ref):
    near = near_ref[...]
    keys = jnp.dot(near, near_weight_ref[...], preferred_element_type=jnp.float32)
    keys += jnp.dot(far_ref[:, 0:BLOCK], far_weight_ref[...], preferred_element_type=jnp.float32)
    keys_ref[...] = (keys * INV_ROOT).astype(jnp.bfloat16)
    gradient = transposed_dot(near, far_ref[:, BLOCK : BLOCK + KVW]) * INV_ROOT
    stepped_ref[...] = near_weight_ref[...].astype(jnp.float32) - inner_rate * gradient


def near_work(far, near, near_weight, far_weight):
    tokens = far.shape[0]
    return pl.pallas_call(
        near_kernel,
        out_shape=[
            jax.ShapeDtypeStruct((tokens, KVW), jnp.bfloat16),
            jax.ShapeDtypeStruct((BLOCK, KVW), jnp.float32),
        ],
        in_specs=[pl.BlockSpec(memory_space=pltpu.VMEM)] * 4,
        out_specs=[pl.BlockSpec(memory_space=pltpu.VMEM)] * 2,
        compiler_params=pltpu.CompilerParams(vmem_limit_bytes=48 * 1024 * 1024),
        name="near_work",
    )(far, near, near_weight, far_weight)


def exchange(rows, axis, groups):
    return lax.all_to_all(rows, axis, split_axis=0, concat_axis=0, tiled=True, axis_index_groups=groups)


def sum_parts(rows, parts):
    stacked = rows.reshape(parts, rows.shape[0] // parts, rows.shape[1])
    return jnp.sum(stacked.astype(jnp.float32), axis=0)


def delta_sum(delta):
    along_x = sum_parts(exchange(delta, "replica", ALONG_X), 4).astype(jnp.bfloat16)
    total = sum_parts(exchange(along_x, "replica", ALONG_Z), 8).astype(jnp.bfloat16)
    spread_z = exchange(jnp.tile(total, (8, 1)), "replica", ALONG_Z)
    return exchange(jnp.tile(spread_z, (4, 1)), "replica", ALONG_X).astype(jnp.float32)


def place_fragment(global_new, start, kv_width):
    placed = jnp.zeros((global_new.shape[0], kv_width), global_new.dtype)
    placed = lax.dynamic_update_slice(placed, global_new, (jnp.zeros((), jnp.int32), start))
    column = lax.broadcasted_iota(jnp.int32, (1, kv_width), 1) - start
    inside = (column >= 0) & (column < global_new.shape[1])
    return (placed, inside)


def body(
    acts,
    norm_gain,
    key_weight,
    key_cotangent,
    pending_delta,
    fragment_index,
    global_frag,
    outer_mom,
):
    weight = key_weight[0]
    far_weight = lax.ppermute(weight, "fsdp", ACROSS)
    half = (lax.axis_index("fsdp") // HALF).astype(jnp.int32).reshape(1)
    far, near = normalise(half, acts, norm_gain.reshape(1, D), key_cotangent)

    far = exchange(far.reshape(HALF * ROWS_IN, BLOCK + KVW), "fsdp", HALVES)
    sent = far_gradient(far)
    arrived = lax.ppermute(sent, "fsdp", ACROSS)

    near, _ = lax.optimization_barrier((near, sent))
    near = exchange(near.reshape(HALF * ROWS_IN, BLOCK), "fsdp", HALVES)
    keys, stepped = near_work(far, near, weight, far_weight)
    key_out = sum_parts(exchange(keys, "fsdp", HALVES), HALF).astype(jnp.bfloat16)

    replicas = lax.axis_size("replica")
    mean_delta = delta_sum(pending_delta[0]) / replicas
    mom_new = momentum_coef * outer_mom + mean_delta
    global_new = global_frag - outer_rate * (momentum_coef * mom_new + mean_delta)
    placed, in_fragment = place_fragment(global_new, fragment_index[0], KVW)

    stepped, placed = lax.optimization_barrier((stepped, placed))
    stepped = stepped - inner_rate * arrived.astype(jnp.float32)
    blended = jnp.where(in_fragment, blend_coef * stepped + (1.0 - blend_coef) * placed, stepped)
    new_weight = blended.astype(jnp.bfloat16)[None]
    return (key_out, new_weight, global_new, mom_new)


def solution(mesh):
    in_specs = (
        P(("replica", "fsdp"), None),
        P(),
        P("replica", "fsdp", None),
        P(("replica", "fsdp"), None),
        P("replica", "fsdp", None),
        P(),
        P("fsdp", None),
        P("fsdp", None),
    )
    out_specs = (
        P(("replica", "fsdp"), None),
        P("replica", "fsdp", None),
        P("fsdp", None),
        P("fsdp", None),
    )
    return jax.shard_map(body, mesh=mesh, in_specs=in_specs, out_specs=out_specs, check_vma=False)
```

```python
import jax
import jax.numpy as jnp
from jax import lax
from jax.experimental import pallas as pl
from jax.experimental.pallas import tpu as pltpu
from jax.sharding import PartitionSpec as P

D = 8192
HALF = 8
PARTS = 16
ROWS_IN = 128
BLOCK = 512
KVW = 512
HD = 128
REPLICAS = 32
INV_ROOT = D ** (-0.5)

inner_rate = 0.5
outer_rate = 0.7
momentum_coef = 0.9
blend_coef = 0.5

HALVES = [list(range(0, HALF)), list(range(HALF, PARTS))]
ALONG_X = [[x * 8 + z for x in range(4)] for z in range(8)]
ALONG_Z = [[x * 8 + z for z in range(8)] for x in range(4)]
ACROSS = [(f, f ^ HALF) for f in range(PARTS)]

TOK = 32
NEAR = 0
FAR = BLOCK
COT = 2 * BLOCK
WIDE = 2 * BLOCK + KVW


def norm_kernel(half_ref, acts_ref, gain_ref, cot_ref, out_ref):
    half = half_ref[0]
    rows = acts_ref[...].astype(jnp.float32)
    scale = lax.rsqrt(jnp.mean(rows * rows, axis=-1, keepdims=True) + 1e-05)
    cot = cot_ref[...]
    span = HALF * BLOCK
    for j in range(HALF):
        for which, slot in ((half, NEAR), (1 - half, FAR)):
            at = pl.ds(pl.multiple_of(which * span + j * BLOCK, BLOCK), BLOCK)
            part = acts_ref[:, at].astype(jnp.float32) * scale * gain_ref[:, at].astype(jnp.float32)
            out_ref[j, :, slot : slot + BLOCK] = part.astype(jnp.bfloat16)
        out_ref[j, :, COT : COT + KVW] = cot


def normalise(half, acts, gain, cot):
    return pl.pallas_call(
        norm_kernel,
        grid_spec=pltpu.PrefetchScalarGridSpec(
            num_scalar_prefetch=1,
            grid=(ROWS_IN // TOK,),
            in_specs=[
                pl.BlockSpec((TOK, D), lambda i, h: (i, 0)),
                pl.BlockSpec((1, D), lambda i, h: (0, 0)),
                pl.BlockSpec((TOK, KVW), lambda i, h: (i, 0)),
            ],
            out_specs=pl.BlockSpec((HALF, TOK, WIDE), lambda i, h: (0, i, 0)),
        ),
        out_shape=jax.ShapeDtypeStruct((HALF, ROWS_IN, WIDE), jnp.bfloat16),
        compiler_params=pltpu.CompilerParams(vmem_limit_bytes=32 * 1024 * 1024),
        name="normalise",
    )(half, acts, gain, cot)


def transposed_dot(left, right):
    return lax.dot_general(left, right, (((0,), (0,)), ((), ())), preferred_element_type=jnp.float32)


def far_kernel(normed_ref, cot_ref, out_ref):
    out_ref[...] = (transposed_dot(normed_ref[...], cot_ref[...]) * INV_ROOT).astype(jnp.bfloat16)


def far_gradient(mixed):
    tokens = mixed.shape[0]
    step = 256
    return pl.pallas_call(
        far_kernel,
        grid=(BLOCK // step,),
        in_specs=[
            pl.BlockSpec((tokens, step), lambda i: (0, FAR // step + i)),
            pl.BlockSpec((tokens, KVW), lambda i: (0, COT // KVW)),
        ],
        out_specs=pl.BlockSpec((step, KVW), lambda i: (i, 0)),
        out_shape=jax.ShapeDtypeStruct((BLOCK, KVW), jnp.bfloat16),
        compiler_params=pltpu.CompilerParams(vmem_limit_bytes=32 * 1024 * 1024),
        name="far_gradient",
    )(mixed, mixed)


def near_kernel(mixed_ref, near_weight_ref, far_weight_ref, keys_ref, stepped_ref):
    near = mixed_ref[:, NEAR : NEAR + BLOCK]
    keys = jnp.dot(near, near_weight_ref[...], preferred_element_type=jnp.float32)
    keys += jnp.dot(mixed_ref[:, FAR : FAR + BLOCK], far_weight_ref[...], preferred_element_type=jnp.float32)
    keys_ref[...] = (keys * INV_ROOT).astype(jnp.bfloat16)
    gradient = transposed_dot(near, mixed_ref[:, COT : COT + KVW]) * INV_ROOT
    stepped_ref[...] = near_weight_ref[...].astype(jnp.float32) - inner_rate * gradient


def near_work(mixed, near_weight, far_weight):
    tokens = mixed.shape[0]
    return pl.pallas_call(
        near_kernel,
        out_shape=[
            jax.ShapeDtypeStruct((tokens, KVW), jnp.bfloat16),
            jax.ShapeDtypeStruct((BLOCK, KVW), jnp.float32),
        ],
        in_specs=[pl.BlockSpec(memory_space=pltpu.VMEM)] * 3,
        out_specs=[pl.BlockSpec(memory_space=pltpu.VMEM)] * 2,
        compiler_params=pltpu.CompilerParams(vmem_limit_bytes=48 * 1024 * 1024),
        name="near_work",
    )(mixed, near_weight, far_weight)


def blend_kernel(start_ref, stepped_ref, arrived_ref, ours_ref, theirs_ref, frag_ref, mom_ref, out_ref, global_ref, mom_new_ref):
    start = start_ref[0]
    mean = (ours_ref[...].astype(jnp.float32) + theirs_ref[...].astype(jnp.float32)) * (1.0 / REPLICAS)
    mom_new = momentum_coef * mom_ref[...] + mean
    global_new = frag_ref[...] - outer_rate * (momentum_coef * mom_new + mean)
    mom_new_ref[...] = mom_new
    global_ref[...] = global_new
    stepped = stepped_ref[...] - inner_rate * arrived_ref[...].astype(jnp.float32)
    wide = jnp.concatenate([global_new, jnp.zeros((global_new.shape[0], KVW - HD), jnp.float32)], axis=1)
    placed = pltpu.roll(wide, start, 1)
    column = lax.broadcasted_iota(jnp.int32, placed.shape, 1) - start
    inside = (column >= 0) & (column < HD)
    blended = jnp.where(inside, blend_coef * stepped + (1.0 - blend_coef) * placed, stepped)
    out_ref[...] = blended.astype(jnp.bfloat16)


def blend(start, stepped, arrived, ours, theirs, frag, mom):
    step = 128
    wide = pl.BlockSpec((step, KVW), lambda i, s: (i, 0))
    slim = pl.BlockSpec((step, HD), lambda i, s: (i, 0))
    return pl.pallas_call(
        blend_kernel,
        grid_spec=pltpu.PrefetchScalarGridSpec(
            num_scalar_prefetch=1,
            grid=(BLOCK // step,),
            in_specs=[wide, wide, slim, slim, slim, slim],
            out_specs=[wide, slim, slim],
        ),
        out_shape=[
            jax.ShapeDtypeStruct((BLOCK, KVW), jnp.bfloat16),
            jax.ShapeDtypeStruct((BLOCK, HD), jnp.float32),
            jax.ShapeDtypeStruct((BLOCK, HD), jnp.float32),
        ],
        compiler_params=pltpu.CompilerParams(vmem_limit_bytes=32 * 1024 * 1024),
        name="blend",
    )(start, stepped, arrived, ours, theirs, frag, mom)


def staged(go, work, *operands):
    shapes = jax.eval_shape(work, *operands)
    skip = lambda *_: jax.tree.map(lambda leaf: jnp.zeros(leaf.shape, leaf.dtype), shapes)
    return lax.cond(go, work, skip, *operands)


def exchange(rows, axis, groups):
    return lax.all_to_all(rows, axis, split_axis=0, concat_axis=0, tiled=True, axis_index_groups=groups)


def sum_parts(rows, parts):
    stacked = rows.reshape(parts, rows.shape[0] // parts, rows.shape[1])
    return jnp.sum(stacked.astype(jnp.float32), axis=0)


def turned(rows, by):
    ring = [(x * 8 + z, ((x + by) % 4) * 8 + z) for x in range(4) for z in range(8)]
    return lax.ppermute(rows, "replica", ring)


def paired(rows, bits):
    return lax.ppermute(rows, "replica", [(r, r ^ bits) for r in range(REPLICAS)])


def own_x():
    return lax.axis_index("replica") // 8


def reduce_x(delta):
    part = delta.shape[0] // 4
    x = own_x()
    pick = lambda by: lax.dynamic_slice_in_dim(delta, lax.rem(x + by, 4) * part, part)
    total = pick(0).astype(jnp.float32)
    for arrived in [turned(pick(by), by) for by in range(1, 4)]:
        total += arrived.astype(jnp.float32)
    return total.astype(jnp.bfloat16)


def spread_x(total):
    blocks = [total] + [turned(total, by) for by in range(1, 4)]
    x = own_x()
    out = jnp.zeros((4 * total.shape[0], total.shape[1]), total.dtype)
    for by in range(4):
        at = lax.rem(x + 4 - by, 4) * total.shape[0]
        out = lax.dynamic_update_slice_in_dim(out, blocks[by], at, 0)
    return out


def body(
    acts,
    norm_gain,
    key_weight,
    key_cotangent,
    pending_delta,
    fragment_index,
    global_frag,
    outer_mom,
):
    weight = key_weight[0]
    go = fragment_index[0] >= 0
    far_weight = lax.ppermute(weight, "fsdp", ACROSS)

    def first(acts, gain, cot, delta):
        half = (lax.axis_index("fsdp") // HALF).astype(jnp.int32).reshape(1)
        mixed = normalise(half, acts, gain.reshape(1, D), cot)
        delta, mixed = lax.optimization_barrier((delta, mixed))
        mixed = exchange(mixed.reshape(HALF * ROWS_IN, WIDE), "fsdp", HALVES)
        own = staged(go, reduce_x, delta)
        arrivals = [paired(own, bits) for bits in (2, 4, 6)]
        sent = far_gradient(mixed)
        arrivals, own, sent = lax.optimization_barrier((arrivals, own, sent))
        total = own.astype(jnp.float32)
        for arrived in arrivals:
            total += arrived.astype(jnp.float32)
        return mixed, total.astype(jnp.bfloat16), sent

    mixed, some, sent = staged(go, first, acts, norm_gain, key_cotangent, pending_delta[0])
    arrived = lax.ppermute(sent, "fsdp", ACROSS)

    def second(mixed, some, weight, far_weight):
        keys, stepped = near_work(mixed, weight, far_weight)
        return keys, stepped, spread_x(some)

    keys, stepped, ours = staged(go, second, mixed, some, weight, far_weight)
    theirs = paired(ours, 1)

    def third(keys):
        return sum_parts(exchange(keys, "fsdp", HALVES), HALF).astype(jnp.bfloat16)

    key_out = staged(go, third, keys)
    key_out, arrived, theirs = lax.optimization_barrier((key_out, arrived, theirs))
    new_weight, global_new, mom_new = blend(fragment_index, stepped, arrived, ours, theirs, global_frag, outer_mom)
    return (key_out, new_weight[None], global_new, mom_new)


def solution(mesh):
    in_specs = (
        P(("replica", "fsdp"), None),
        P(),
        P("replica", "fsdp", None),
        P(("replica", "fsdp"), None),
        P("replica", "fsdp", None),
        P(),
        P("fsdp", None),
        P("fsdp", None),
    )
    out_specs = (
        P(("replica", "fsdp"), None),
        P("replica", "fsdp", None),
        P("fsdp", None),
        P("fsdp", None),
    )
    return jax.shard_map(body, mesh=mesh, in_specs=in_specs, out_specs=out_specs, check_vma=False)
```

```python
import jax
import jax.numpy as jnp
from jax import lax
from jax.experimental import pallas as pl
from jax.experimental.pallas import tpu as pltpu
from jax.sharding import PartitionSpec as P

D = 8192
HALF = 8
PARTS = 16
ROWS_IN = 128
BLOCK = 512
KVW = 512
HD = 128
JOIN_COST = pl.CostEstimate(flops=11500000000, bytes_accessed=10**6, transcendentals=0)
HOLD_COST = pl.CostEstimate(flops=26450000000, bytes_accessed=10**6, transcendentals=0)
SHORT = pl.CostEstimate(flops=10**6, bytes_accessed=10**4, transcendentals=0)
REPLICAS = 32
INV_ROOT = D ** (-0.5)

inner_rate = 0.5
outer_rate = 0.7
momentum_coef = 0.9
blend_coef = 0.5

HALVES = [list(range(0, HALF)), list(range(HALF, PARTS))]
ALONG_X = [[x * 8 + z for x in range(4)] for z in range(8)]
ALONG_Z = [[x * 8 + z for z in range(8)] for x in range(4)]
ACROSS = [(f, f ^ HALF) for f in range(PARTS)]

TOK = 32
NEAR = 0
FAR = BLOCK
COT = 2 * BLOCK
WIDE = 2 * BLOCK + KVW


def norm_kernel(half_ref, acts_ref, gain_ref, cot_ref, out_ref):
    half = half_ref[0]
    rows = acts_ref[...].astype(jnp.float32)
    scale = lax.rsqrt(jnp.mean(rows * rows, axis=-1, keepdims=True) + 1e-05)
    cot = cot_ref[...]
    span = HALF * BLOCK
    for j in range(HALF):
        for which, slot in ((half, NEAR), (1 - half, FAR)):
            at = pl.ds(pl.multiple_of(which * span + j * BLOCK, BLOCK), BLOCK)
            part = acts_ref[:, at].astype(jnp.float32) * scale * gain_ref[:, at].astype(jnp.float32)
            out_ref[j, :, slot : slot + BLOCK] = part.astype(jnp.bfloat16)
        out_ref[j, :, COT : COT + KVW] = cot


def normalise(half, acts, gain, cot):
    return pl.pallas_call(
        norm_kernel,
        grid_spec=pltpu.PrefetchScalarGridSpec(
            num_scalar_prefetch=1,
            grid=(ROWS_IN // TOK,),
            in_specs=[
                pl.BlockSpec((TOK, D), lambda i, h: (i, 0)),
                pl.BlockSpec((1, D), lambda i, h: (0, 0)),
                pl.BlockSpec((TOK, KVW), lambda i, h: (i, 0)),
            ],
            out_specs=pl.BlockSpec((HALF, TOK, WIDE), lambda i, h: (0, i, 0)),
        ),
        out_shape=jax.ShapeDtypeStruct((HALF, ROWS_IN, WIDE), jnp.bfloat16),
        compiler_params=pltpu.CompilerParams(vmem_limit_bytes=32 * 1024 * 1024),
        cost_estimate=SHORT,
        name="normalise",
    )(half, acts, gain, cot)


def transposed_dot(left, right):
    return lax.dot_general(left, right, (((0,), (0,)), ((), ())), preferred_element_type=jnp.float32)


def far_kernel(normed_ref, cot_ref, out_ref):
    out_ref[...] = (transposed_dot(normed_ref[...], cot_ref[...]) * INV_ROOT).astype(jnp.bfloat16)


def far_gradient(mixed):
    tokens = mixed.shape[0]
    step = 256
    return pl.pallas_call(
        far_kernel,
        grid=(BLOCK // step,),
        in_specs=[
            pl.BlockSpec((tokens, step), lambda i: (0, FAR // step + i)),
            pl.BlockSpec((tokens, KVW), lambda i: (0, COT // KVW)),
        ],
        out_specs=pl.BlockSpec((step, KVW), lambda i: (i, 0)),
        out_shape=jax.ShapeDtypeStruct((BLOCK, KVW), jnp.bfloat16),
        compiler_params=pltpu.CompilerParams(vmem_limit_bytes=32 * 1024 * 1024),
        cost_estimate=SHORT,
        name="far_gradient",
    )(mixed, mixed)


def near_kernel(mixed_ref, near_weight_ref, far_weight_ref, keys_ref, stepped_ref):
    near = mixed_ref[:, NEAR : NEAR + BLOCK]
    keys = jnp.dot(near, near_weight_ref[...], preferred_element_type=jnp.float32)
    keys += jnp.dot(mixed_ref[:, FAR : FAR + BLOCK], far_weight_ref[...], preferred_element_type=jnp.float32)
    keys_ref[...] = (keys * INV_ROOT).astype(jnp.bfloat16)
    gradient = transposed_dot(near, mixed_ref[:, COT : COT + KVW]) * INV_ROOT
    stepped_ref[...] = near_weight_ref[...].astype(jnp.float32) - inner_rate * gradient


def near_work(mixed, near_weight, far_weight):
    tokens = mixed.shape[0]
    return pl.pallas_call(
        near_kernel,
        out_shape=[
            jax.ShapeDtypeStruct((tokens, KVW), jnp.bfloat16),
            jax.ShapeDtypeStruct((BLOCK, KVW), jnp.float32),
        ],
        in_specs=[pl.BlockSpec(memory_space=pltpu.VMEM)] * 3,
        out_specs=[pl.BlockSpec(memory_space=pltpu.VMEM)] * 2,
        compiler_params=pltpu.CompilerParams(vmem_limit_bytes=48 * 1024 * 1024),
        name="near_work",
    )(mixed, near_weight, far_weight)


def blend_kernel(start_ref, stepped_ref, arrived_ref, ours_ref, theirs_ref, frag_ref, mom_ref, out_ref, global_ref, mom_new_ref):
    start = start_ref[0]
    mean = (ours_ref[...].astype(jnp.float32) + theirs_ref[...].astype(jnp.float32)) * (1.0 / REPLICAS)
    mom_new = momentum_coef * mom_ref[...] + mean
    global_new = frag_ref[...] - outer_rate * (momentum_coef * mom_new + mean)
    mom_new_ref[...] = mom_new
    global_ref[...] = global_new
    stepped = stepped_ref[...] - inner_rate * arrived_ref[...].astype(jnp.float32)
    wide = jnp.concatenate([global_new, jnp.zeros((global_new.shape[0], KVW - HD), jnp.float32)], axis=1)
    placed = pltpu.roll(wide, start, 1)
    column = lax.broadcasted_iota(jnp.int32, placed.shape, 1) - start
    inside = (column >= 0) & (column < HD)
    blended = jnp.where(inside, blend_coef * stepped + (1.0 - blend_coef) * placed, stepped)
    out_ref[...] = blended.astype(jnp.bfloat16)


def blend(start, stepped, arrived, ours, theirs, frag, mom):
    step = 128
    wide = pl.BlockSpec((step, KVW), lambda i, s: (i, 0))
    slim = pl.BlockSpec((step, HD), lambda i, s: (i, 0))
    return pl.pallas_call(
        blend_kernel,
        grid_spec=pltpu.PrefetchScalarGridSpec(
            num_scalar_prefetch=1,
            grid=(BLOCK // step,),
            in_specs=[wide, wide, slim, slim, slim, slim],
            out_specs=[wide, slim, slim],
        ),
        out_shape=[
            jax.ShapeDtypeStruct((BLOCK, KVW), jnp.bfloat16),
            jax.ShapeDtypeStruct((BLOCK, HD), jnp.float32),
            jax.ShapeDtypeStruct((BLOCK, HD), jnp.float32),
        ],
        compiler_params=pltpu.CompilerParams(vmem_limit_bytes=32 * 1024 * 1024),
        name="blend",
    )(start, stepped, arrived, ours, theirs, frag, mom)


def staged(go, work, *operands):
    shapes = jax.eval_shape(work, *operands)
    skip = lambda *_: jax.tree.map(lambda leaf: jnp.zeros(leaf.shape, leaf.dtype), shapes)
    return lax.cond(go, work, skip, *operands)


def exchange(rows, axis, groups):
    return lax.all_to_all(rows, axis, split_axis=0, concat_axis=0, tiled=True, axis_index_groups=groups)


def sum_parts(rows, parts):
    stacked = rows.reshape(parts, rows.shape[0] // parts, rows.shape[1])
    return jnp.sum(stacked.astype(jnp.float32), axis=0)


def turned(rows, by):
    ring = [(x * 8 + z, ((x + by) % 4) * 8 + z) for x in range(4) for z in range(8)]
    return lax.ppermute(rows, "replica", ring)


def paired(rows, bits):
    return lax.ppermute(rows, "replica", [(r, r ^ bits) for r in range(REPLICAS)])


def own_x():
    return lax.axis_index("replica") // 8


def reduce_x(delta):
    part = delta.shape[0] // 4
    x = own_x()
    pick = lambda by: lax.dynamic_slice_in_dim(delta, lax.rem(x + by, 4) * part, part)
    total = pick(0).astype(jnp.float32)
    for arrived in [turned(pick(by), by) for by in range(1, 4)]:
        total += arrived.astype(jnp.float32)
    return total.astype(jnp.bfloat16)


def hold_kernel(in_ref, out_ref):
    out_ref[...] = in_ref[...]


def hold(rows):
    return pl.pallas_call(
        hold_kernel,
        out_shape=jax.ShapeDtypeStruct(rows.shape, rows.dtype),
        in_specs=[pl.BlockSpec(memory_space=pltpu.VMEM)],
        out_specs=pl.BlockSpec(memory_space=pltpu.VMEM),
        compiler_params=pltpu.CompilerParams(vmem_limit_bytes=16 * 1024 * 1024),
        cost_estimate=HOLD_COST,
        name="hold",
    )(rows)


def join_kernel(x_ref, a_ref, b_ref, c_ref, d_ref, out_ref):
    x = x_ref[0]
    part = a_ref.shape[0]
    for by, ref in enumerate((a_ref, b_ref, c_ref, d_ref)):
        at = pl.multiple_of(lax.rem(x + 4 - by, 4) * part, part)
        out_ref[pl.ds(at, part), :] = ref[...]


def join(blocks):
    part, width = blocks[0].shape
    return pl.pallas_call(
        join_kernel,
        out_shape=jax.ShapeDtypeStruct((4 * part, width), jnp.bfloat16),
        in_specs=[pl.BlockSpec(memory_space=pltpu.SMEM)] + [pl.BlockSpec(memory_space=pltpu.VMEM)] * 4,
        out_specs=pl.BlockSpec(memory_space=pltpu.VMEM),
        compiler_params=pltpu.CompilerParams(vmem_limit_bytes=16 * 1024 * 1024),
        cost_estimate=JOIN_COST,
        name="join",
    )(own_x().astype(jnp.int32).reshape(1), *blocks)


def body(
    acts,
    norm_gain,
    key_weight,
    key_cotangent,
    pending_delta,
    fragment_index,
    global_frag,
    outer_mom,
):
    weight = key_weight[0]
    go = fragment_index[0] >= 0
    far_weight = lax.ppermute(weight, "fsdp", ACROSS)

    half = (lax.axis_index("fsdp") // HALF).astype(jnp.int32).reshape(1)
    mixed = normalise(half, acts, norm_gain.reshape(1, D), key_cotangent)
    delta, mixed = lax.optimization_barrier((pending_delta[0], mixed))
    mixed = exchange(mixed.reshape(HALF * ROWS_IN, WIDE), "fsdp", HALVES)
    own = staged(go, reduce_x, delta)
    arrivals = [paired(own, bits) for bits in (2, 4, 6)]
    far_weight = hold(far_weight)
    mixed, far_weight = lax.optimization_barrier((mixed, far_weight))
    sent = far_gradient(mixed)
    arrived = lax.ppermute(sent, "fsdp", ACROSS)

    def second(mixed, own, arrivals, weight, far_weight):
        some = own.astype(jnp.float32)
        for part in arrivals:
            some += part.astype(jnp.float32)
        some = some.astype(jnp.bfloat16)
        blocks = [some] + [turned(some, by) for by in range(1, 4)]
        keys, stepped = near_work(mixed, weight, far_weight)
        return keys, stepped, blocks

    keys, stepped, blocks = staged(go, second, mixed, own, arrivals, weight, far_weight)
    ours = join(blocks)
    keys, ours = lax.optimization_barrier((keys, ours))
    theirs = paired(ours, 1)

    def third(keys):
        return sum_parts(exchange(keys, "fsdp", HALVES), HALF).astype(jnp.bfloat16)

    key_out = staged(go, third, keys)
    key_out, arrived, theirs = lax.optimization_barrier((key_out, arrived, theirs))
    new_weight, global_new, mom_new = blend(fragment_index, stepped, arrived, ours, theirs, global_frag, outer_mom)
    return (key_out, new_weight[None], global_new, mom_new)


def solution(mesh):
    in_specs = (
        P(("replica", "fsdp"), None),
        P(),
        P("replica", "fsdp", None),
        P(("replica", "fsdp"), None),
        P("replica", "fsdp", None),
        P(),
        P("fsdp", None),
        P("fsdp", None),
    )
    out_specs = (
        P(("replica", "fsdp"), None),
        P("replica", "fsdp", None),
        P("fsdp", None),
        P("fsdp", None),
    )
    return jax.shard_map(body, mesh=mesh, in_specs=in_specs, out_specs=out_specs, check_vma=False)
```

```python
import jax
import jax.numpy as jnp
from jax import lax
from jax.experimental import pallas as pl
from jax.experimental.pallas import tpu as pltpu
from jax.sharding import PartitionSpec as P

D = 8192
HALF = 8
PARTS = 16
ROWS_IN = 128
BLOCK = 512
KVW = 512
HD = 128
JOIN_COST = pl.CostEstimate(flops=11500000000, bytes_accessed=10**6, transcendentals=0)
HOLD_COST = pl.CostEstimate(flops=26450000000, bytes_accessed=10**6, transcendentals=0)
SHORT = pl.CostEstimate(flops=10**6, bytes_accessed=10**4, transcendentals=0)
REPLICAS = 32
INV_ROOT = D ** (-0.5)

inner_rate = 0.5
outer_rate = 0.7
momentum_coef = 0.9
blend_coef = 0.5

HALVES = [list(range(0, HALF)), list(range(HALF, PARTS))]
ALONG_X = [[x * 8 + z for x in range(4)] for z in range(8)]
ALONG_Z = [[x * 8 + z for z in range(8)] for x in range(4)]
ACROSS = [(f, f ^ HALF) for f in range(PARTS)]

TOK = 64
LANES = 128
NORM_VMEM = 60 * 1024 * 1024
NEAR = 0
FAR = BLOCK
COT = 2 * BLOCK
WIDE = 2 * BLOCK + KVW


def norm_kernel(half_ref, acts_ref, gain_ref, cot_ref, out_ref):
    rows = acts_ref[...].astype(jnp.float32)
    scale = lax.rsqrt(jnp.mean(rows * rows, axis=-1, keepdims=True) + 1e-05)
    gain = gain_ref[...].astype(jnp.float32)
    cot = cot_ref[...]
    span = HALF * BLOCK
    for half in range(2):

        @pl.when(half_ref[0] == half)
        def _():
            for which, slot in ((half, NEAR), (1 - half, FAR)):
                for j in range(HALF):
                    for k in range(0, BLOCK, LANES):
                        start = which * span + j * BLOCK + k
                        row = start // LANES
                        part = acts_ref[:, start : start + LANES].astype(jnp.float32) * scale * gain[row : row + 1, :]
                        out_ref[j, :, slot + k : slot + k + LANES] = part.astype(jnp.bfloat16)

    for j in range(HALF):
        out_ref[j, :, COT : COT + KVW] = cot


def normalise(half, acts, gain, cot):
    return pl.pallas_call(
        norm_kernel,
        grid_spec=pltpu.PrefetchScalarGridSpec(
            num_scalar_prefetch=1,
            grid=(ROWS_IN // TOK,),
            in_specs=[
                pl.BlockSpec((TOK, D), lambda i, h: (i, 0)),
                pl.BlockSpec((D // LANES, LANES), lambda i, h: (0, 0)),
                pl.BlockSpec((TOK, KVW), lambda i, h: (i, 0)),
            ],
            out_specs=pl.BlockSpec((HALF, TOK, WIDE), lambda i, h: (0, i, 0)),
        ),
        out_shape=jax.ShapeDtypeStruct((HALF, ROWS_IN, WIDE), jnp.bfloat16),
        compiler_params=pltpu.CompilerParams(vmem_limit_bytes=NORM_VMEM),
        cost_estimate=SHORT,
        name="normalise",
    )(half, acts, gain, cot)


def transposed_dot(left, right):
    return lax.dot_general(left, right, (((0,), (0,)), ((), ())), preferred_element_type=jnp.float32)


def far_kernel(normed_ref, cot_ref, _, out_ref):
    out_ref[...] = (transposed_dot(normed_ref[...], cot_ref[...]) * INV_ROOT).astype(jnp.bfloat16)


def far_gradient(mixed, after):
    tokens = mixed.shape[0]
    step = 256
    return pl.pallas_call(
        far_kernel,
        grid=(BLOCK // step,),
        in_specs=[
            pl.BlockSpec((tokens, step), lambda i: (0, FAR // step + i)),
            pl.BlockSpec((tokens, KVW), lambda i: (0, COT // KVW)),
            pl.BlockSpec(memory_space=pl.ANY),
        ],
        out_specs=pl.BlockSpec((step, KVW), lambda i: (i, 0)),
        out_shape=jax.ShapeDtypeStruct((BLOCK, KVW), jnp.bfloat16),
        compiler_params=pltpu.CompilerParams(vmem_limit_bytes=32 * 1024 * 1024),
        cost_estimate=SHORT,
        name="far_gradient",
    )(mixed, mixed, after)


def near_kernel(mixed_ref, near_weight_ref, far_weight_ref, keys_ref, stepped_ref):
    near = mixed_ref[:, NEAR : NEAR + BLOCK]
    keys = jnp.dot(near, near_weight_ref[...], preferred_element_type=jnp.float32)
    keys += jnp.dot(mixed_ref[:, FAR : FAR + BLOCK], far_weight_ref[...], preferred_element_type=jnp.float32)
    keys_ref[...] = (keys * INV_ROOT).astype(jnp.bfloat16)
    gradient = transposed_dot(near, mixed_ref[:, COT : COT + KVW]) * INV_ROOT
    stepped_ref[...] = near_weight_ref[...].astype(jnp.float32) - inner_rate * gradient


def near_work(mixed, near_weight, far_weight):
    tokens = mixed.shape[0]
    return pl.pallas_call(
        near_kernel,
        out_shape=[
            jax.ShapeDtypeStruct((tokens, KVW), jnp.bfloat16),
            jax.ShapeDtypeStruct((BLOCK, KVW), jnp.float32),
        ],
        in_specs=[pl.BlockSpec(memory_space=pltpu.VMEM)] * 3,
        out_specs=[pl.BlockSpec(memory_space=pltpu.VMEM)] * 2,
        compiler_params=pltpu.CompilerParams(vmem_limit_bytes=48 * 1024 * 1024),
        name="near_work",
    )(mixed, near_weight, far_weight)


def blend_kernel(start_ref, stepped_ref, arrived_ref, ours_ref, theirs_ref, frag_ref, mom_ref, out_ref, global_ref, mom_new_ref):
    start = start_ref[0]
    mean = (ours_ref[...].astype(jnp.float32) + theirs_ref[...].astype(jnp.float32)) * (1.0 / REPLICAS)
    mom_new = momentum_coef * mom_ref[...] + mean
    global_new = frag_ref[...] - outer_rate * (momentum_coef * mom_new + mean)
    mom_new_ref[...] = mom_new
    global_ref[...] = global_new
    stepped = stepped_ref[...] - inner_rate * arrived_ref[...].astype(jnp.float32)
    wide = jnp.concatenate([global_new, jnp.zeros((global_new.shape[0], KVW - HD), jnp.float32)], axis=1)
    placed = pltpu.roll(wide, start, 1)
    column = lax.broadcasted_iota(jnp.int32, placed.shape, 1) - start
    inside = (column >= 0) & (column < HD)
    blended = jnp.where(inside, blend_coef * stepped + (1.0 - blend_coef) * placed, stepped)
    out_ref[...] = blended.astype(jnp.bfloat16)


def blend(start, stepped, arrived, ours, theirs, frag, mom):
    return pl.pallas_call(
        blend_kernel,
        in_specs=[pl.BlockSpec(memory_space=pltpu.SMEM)] + [pl.BlockSpec(memory_space=pltpu.VMEM)] * 6,
        out_specs=[pl.BlockSpec(memory_space=pltpu.VMEM)] * 3,
        out_shape=[
            jax.ShapeDtypeStruct((BLOCK, KVW), jnp.bfloat16),
            jax.ShapeDtypeStruct((BLOCK, HD), jnp.float32),
            jax.ShapeDtypeStruct((BLOCK, HD), jnp.float32),
        ],
        compiler_params=pltpu.CompilerParams(vmem_limit_bytes=24 * 1024 * 1024),
        name="blend",
    )(start, stepped, arrived, ours, theirs, frag, mom)


def staged(go, work, *operands):
    shapes = jax.eval_shape(work, *operands)
    skip = lambda *_: jax.tree.map(lambda leaf: jnp.zeros(leaf.shape, leaf.dtype), shapes)
    return lax.cond(go, work, skip, *operands)


def exchange(rows, axis, groups):
    return lax.all_to_all(rows, axis, split_axis=0, concat_axis=0, tiled=True, axis_index_groups=groups)


def sum_parts(rows, parts):
    stacked = rows.reshape(parts, rows.shape[0] // parts, rows.shape[1])
    return jnp.sum(stacked.astype(jnp.float32), axis=0)


def turned(rows, by):
    ring = [(x * 8 + z, ((x + by) % 4) * 8 + z) for x in range(4) for z in range(8)]
    return lax.ppermute(rows, "replica", ring)


def paired(rows, bits):
    return lax.ppermute(rows, "replica", [(r, r ^ bits) for r in range(REPLICAS)])


def own_x():
    return lax.axis_index("replica") // 8


def reduce_x(delta):
    part = delta.shape[0] // 4
    x = own_x()
    pick = lambda by: lax.dynamic_slice_in_dim(delta, lax.rem(x + by, 4) * part, part)
    total = pick(0).astype(jnp.float32)
    for arrived in [turned(pick(by), by) for by in range(1, 4)]:
        total += arrived.astype(jnp.float32)
    return total.astype(jnp.bfloat16)


def hold_kernel(in_ref, out_ref):
    out_ref[...] = in_ref[...]


def hold(rows):
    return pl.pallas_call(
        hold_kernel,
        grid=(1,),
        in_specs=[pl.BlockSpec((16, LANES), lambda i: (0, 0))],
        out_specs=pl.BlockSpec((16, LANES), lambda i: (0, 0)),
        out_shape=jax.ShapeDtypeStruct((16, LANES), rows.dtype),
        compiler_params=pltpu.CompilerParams(vmem_limit_bytes=16 * 1024 * 1024),
        cost_estimate=HOLD_COST,
        name="hold",
    )(rows)


def join_kernel(x_ref, a_ref, b_ref, c_ref, d_ref, out_ref):
    x = x_ref[0]
    part = a_ref.shape[0]
    for by, ref in enumerate((a_ref, b_ref, c_ref, d_ref)):
        at = pl.multiple_of(lax.rem(x + 4 - by, 4) * part, part)
        out_ref[pl.ds(at, part), :] = ref[...]


def join(blocks):
    part, width = blocks[0].shape
    return pl.pallas_call(
        join_kernel,
        out_shape=jax.ShapeDtypeStruct((4 * part, width), jnp.bfloat16),
        in_specs=[pl.BlockSpec(memory_space=pltpu.SMEM)] + [pl.BlockSpec(memory_space=pltpu.VMEM)] * 4,
        out_specs=pl.BlockSpec(memory_space=pltpu.VMEM),
        compiler_params=pltpu.CompilerParams(vmem_limit_bytes=16 * 1024 * 1024),
        cost_estimate=JOIN_COST,
        name="join",
    )(own_x().astype(jnp.int32).reshape(1), *blocks)


def body(
    acts,
    norm_gain,
    key_weight,
    key_cotangent,
    pending_delta,
    fragment_index,
    global_frag,
    outer_mom,
):
    weight = key_weight[0]
    go = fragment_index[0] >= 0
    far_weight = lax.ppermute(weight, "fsdp", ACROSS)

    half = (lax.axis_index("fsdp") // HALF).astype(jnp.int32).reshape(1)
    mixed = normalise(half, acts, norm_gain.reshape(D // LANES, LANES), key_cotangent)
    delta, mixed = lax.optimization_barrier((pending_delta[0], mixed))
    mixed = exchange(mixed.reshape(HALF * ROWS_IN, WIDE), "fsdp", HALVES)
    own = staged(go, reduce_x, delta)
    arrivals = [paired(own, bits) for bits in (2, 4, 6)]
    sent = far_gradient(mixed, hold(far_weight))
    arrived = lax.ppermute(sent, "fsdp", ACROSS)

    def second(mixed, own, arrivals, weight, far_weight):
        some = own.astype(jnp.float32)
        for part in arrivals:
            some += part.astype(jnp.float32)
        some = some.astype(jnp.bfloat16)
        blocks = [some] + [turned(some, by) for by in range(1, 4)]
        keys, stepped = near_work(mixed, weight, far_weight)
        return keys, stepped, blocks

    keys, stepped, blocks = staged(go, second, mixed, own, arrivals, weight, far_weight)
    ours = join(blocks)
    keys, ours = lax.optimization_barrier((keys, ours))
    theirs = paired(ours, 1)

    def third(keys):
        return sum_parts(exchange(keys, "fsdp", HALVES), HALF).astype(jnp.bfloat16)

    key_out = staged(go, third, keys)
    key_out, arrived, theirs = lax.optimization_barrier((key_out, arrived, theirs))
    new_weight, global_new, mom_new = blend(fragment_index, stepped, arrived, ours, theirs, global_frag, outer_mom)
    return (key_out, new_weight[None], global_new, mom_new)


def solution(mesh):
    in_specs = (
        P(("replica", "fsdp"), None),
        P(),
        P("replica", "fsdp", None),
        P(("replica", "fsdp"), None),
        P("replica", "fsdp", None),
        P(),
        P("fsdp", None),
        P("fsdp", None),
    )
    out_specs = (
        P(("replica", "fsdp"), None),
        P("replica", "fsdp", None),
        P("fsdp", None),
        P("fsdp", None),
    )
    return jax.shard_map(body, mesh=mesh, in_specs=in_specs, out_specs=out_specs, check_vma=False)
```

```python
import jax
import jax.numpy as jnp
from jax import lax
from jax.experimental import pallas as pl
from jax.experimental.pallas import tpu as pltpu
from jax.sharding import PartitionSpec as P

D = 8192
HALF = 8
PARTS = 16
ROWS_IN = 128
BLOCK = 512
KVW = 512
HD = 128
JOIN_COST = pl.CostEstimate(flops=11500000000, bytes_accessed=10**6, transcendentals=0)
HOLD_COST = pl.CostEstimate(flops=26450000000, bytes_accessed=10**6, transcendentals=0)
SHORT = pl.CostEstimate(flops=10**6, bytes_accessed=10**4, transcendentals=0)
REPLICAS = 32
INV_ROOT = D ** (-0.5)

inner_rate = 0.5
outer_rate = 0.7
momentum_coef = 0.9
blend_coef = 0.5

HALVES = [list(range(0, HALF)), list(range(HALF, PARTS))]
ALONG_X = [[x * 8 + z for x in range(4)] for z in range(8)]
ALONG_Z = [[x * 8 + z for z in range(8)] for x in range(4)]
ACROSS = [(f, f ^ HALF) for f in range(PARTS)]

TOK = 64
LANES = 128
NORM_VMEM = 60 * 1024 * 1024
NEAR = 0
FAR = BLOCK
COT = 2 * BLOCK
WIDE = 2 * BLOCK + KVW


def norm_kernel(half_ref, acts_ref, gain_ref, cot_ref, out_ref):
    rows = acts_ref[...].astype(jnp.float32)
    scale = lax.rsqrt(jnp.mean(rows * rows, axis=-1, keepdims=True) + 1e-05)
    gain = gain_ref[...].astype(jnp.float32)
    cot = cot_ref[...]
    span = HALF * BLOCK
    for half in range(2):

        @pl.when(half_ref[0] == half)
        def _():
            for which, slot in ((half, NEAR), (1 - half, FAR)):
                for j in range(HALF):
                    for k in range(0, BLOCK, LANES):
                        start = which * span + j * BLOCK + k
                        row = start // LANES
                        part = acts_ref[:, start : start + LANES].astype(jnp.float32) * scale * gain[row : row + 1, :]
                        out_ref[j, :, slot + k : slot + k + LANES] = part.astype(jnp.bfloat16)

    for j in range(HALF):
        out_ref[j, :, COT : COT + KVW] = cot


def normalise(half, acts, gain, cot):
    return pl.pallas_call(
        norm_kernel,
        grid_spec=pltpu.PrefetchScalarGridSpec(
            num_scalar_prefetch=1,
            grid=(ROWS_IN // TOK,),
            in_specs=[
                pl.BlockSpec((TOK, D), lambda i, h: (i, 0)),
                pl.BlockSpec((D // LANES, LANES), lambda i, h: (0, 0)),
                pl.BlockSpec((TOK, KVW), lambda i, h: (i, 0)),
            ],
            out_specs=pl.BlockSpec((HALF, TOK, WIDE), lambda i, h: (0, i, 0)),
        ),
        out_shape=jax.ShapeDtypeStruct((HALF, ROWS_IN, WIDE), jnp.bfloat16),
        compiler_params=pltpu.CompilerParams(vmem_limit_bytes=NORM_VMEM),
        cost_estimate=SHORT,
        name="normalise",
    )(half, acts, gain, cot)


def transposed_dot(left, right):
    return lax.dot_general(left, right, (((0,), (0,)), ((), ())), preferred_element_type=jnp.float32)


def far_kernel(normed_ref, cot_ref, out_ref):
    out_ref[...] = (transposed_dot(normed_ref[...], cot_ref[...]) * INV_ROOT).astype(jnp.bfloat16)


def far_gradient(mixed):
    tokens = mixed.shape[0]
    step = 256
    return pl.pallas_call(
        far_kernel,
        grid=(BLOCK // step,),
        in_specs=[
            pl.BlockSpec((tokens, step), lambda i: (0, FAR // step + i)),
            pl.BlockSpec((tokens, KVW), lambda i: (0, COT // KVW)),
        ],
        out_specs=pl.BlockSpec((step, KVW), lambda i: (i, 0)),
        out_shape=jax.ShapeDtypeStruct((BLOCK, KVW), jnp.bfloat16),
        compiler_params=pltpu.CompilerParams(vmem_limit_bytes=32 * 1024 * 1024),
        cost_estimate=SHORT,
        name="far_gradient",
    )(mixed, mixed)


def near_kernel(mixed_ref, near_weight_ref, far_weight_ref, keys_ref, stepped_ref):
    near = mixed_ref[:, NEAR : NEAR + BLOCK]
    keys = jnp.dot(near, near_weight_ref[...], preferred_element_type=jnp.float32)
    keys += jnp.dot(mixed_ref[:, FAR : FAR + BLOCK], far_weight_ref[...], preferred_element_type=jnp.float32)
    keys_ref[...] = (keys * INV_ROOT).astype(jnp.bfloat16)
    gradient = transposed_dot(near, mixed_ref[:, COT : COT + KVW]) * INV_ROOT
    stepped_ref[...] = near_weight_ref[...].astype(jnp.float32) - inner_rate * gradient


def near_work(mixed, near_weight, far_weight):
    tokens = mixed.shape[0]
    return pl.pallas_call(
        near_kernel,
        out_shape=[
            jax.ShapeDtypeStruct((tokens, KVW), jnp.bfloat16),
            jax.ShapeDtypeStruct((BLOCK, KVW), jnp.float32),
        ],
        in_specs=[pl.BlockSpec(memory_space=pltpu.VMEM)] * 3,
        out_specs=[pl.BlockSpec(memory_space=pltpu.VMEM)] * 2,
        compiler_params=pltpu.CompilerParams(vmem_limit_bytes=48 * 1024 * 1024),
        name="near_work",
    )(mixed, near_weight, far_weight)


def blend_kernel(start_ref, stepped_ref, arrived_ref, ours_ref, theirs_ref, frag_ref, mom_ref, out_ref, global_ref, mom_new_ref):
    start = start_ref[0]
    mean = (ours_ref[...].astype(jnp.float32) + theirs_ref[...].astype(jnp.float32)) * (1.0 / REPLICAS)
    mom_new = momentum_coef * mom_ref[...] + mean
    global_new = frag_ref[...] - outer_rate * (momentum_coef * mom_new + mean)
    mom_new_ref[...] = mom_new
    global_ref[...] = global_new
    stepped = stepped_ref[...] - inner_rate * arrived_ref[...].astype(jnp.float32)
    wide = jnp.concatenate([global_new, jnp.zeros((global_new.shape[0], KVW - HD), jnp.float32)], axis=1)
    placed = pltpu.roll(wide, start, 1)
    column = lax.broadcasted_iota(jnp.int32, placed.shape, 1) - start
    inside = (column >= 0) & (column < HD)
    blended = jnp.where(inside, blend_coef * stepped + (1.0 - blend_coef) * placed, stepped)
    out_ref[...] = blended.astype(jnp.bfloat16)


def blend(start, stepped, arrived, ours, theirs, frag, mom):
    return pl.pallas_call(
        blend_kernel,
        in_specs=[pl.BlockSpec(memory_space=pltpu.SMEM)] + [pl.BlockSpec(memory_space=pltpu.VMEM)] * 6,
        out_specs=[pl.BlockSpec(memory_space=pltpu.VMEM)] * 3,
        out_shape=[
            jax.ShapeDtypeStruct((BLOCK, KVW), jnp.bfloat16),
            jax.ShapeDtypeStruct((BLOCK, HD), jnp.float32),
            jax.ShapeDtypeStruct((BLOCK, HD), jnp.float32),
        ],
        compiler_params=pltpu.CompilerParams(vmem_limit_bytes=24 * 1024 * 1024),
        name="blend",
    )(start, stepped, arrived, ours, theirs, frag, mom)


def staged(go, work, *operands):
    shapes = jax.eval_shape(work, *operands)
    skip = lambda *_: jax.tree.map(lambda leaf: jnp.zeros(leaf.shape, leaf.dtype), shapes)
    return lax.cond(go, work, skip, *operands)


def exchange(rows, axis, groups):
    return lax.all_to_all(rows, axis, split_axis=0, concat_axis=0, tiled=True, axis_index_groups=groups)


def sum_parts(rows, parts):
    stacked = rows.reshape(parts, rows.shape[0] // parts, rows.shape[1])
    return jnp.sum(stacked.astype(jnp.float32), axis=0)


def turned(rows, by):
    ring = [(x * 8 + z, ((x + by) % 4) * 8 + z) for x in range(4) for z in range(8)]
    return lax.ppermute(rows, "replica", ring)


def paired(rows, bits):
    return lax.ppermute(rows, "replica", [(r, r ^ bits) for r in range(REPLICAS)])


def own_x():
    return lax.axis_index("replica") // 8


def reduce_x(delta):
    part = delta.shape[0] // 4
    x = own_x()
    pick = lambda by: lax.dynamic_slice_in_dim(delta, lax.rem(x + by, 4) * part, part)
    total = pick(0).astype(jnp.float32)
    for arrived in [turned(pick(by), by) for by in range(1, 4)]:
        total += arrived.astype(jnp.float32)
    return total.astype(jnp.bfloat16)


def hold_kernel(in_ref, out_ref):
    out_ref[...] = in_ref[...]


def hold(rows):
    return pl.pallas_call(
        hold_kernel,
        out_shape=jax.ShapeDtypeStruct(rows.shape, rows.dtype),
        in_specs=[pl.BlockSpec(memory_space=pltpu.VMEM)],
        out_specs=pl.BlockSpec(memory_space=pltpu.VMEM),
        compiler_params=pltpu.CompilerParams(vmem_limit_bytes=16 * 1024 * 1024),
        cost_estimate=HOLD_COST,
        name="hold",
    )(rows)


def join_kernel(x_ref, a_ref, b_ref, c_ref, d_ref, out_ref):
    x = x_ref[0]
    part = a_ref.shape[0]
    for by, ref in enumerate((a_ref, b_ref, c_ref, d_ref)):
        at = pl.multiple_of(lax.rem(x + 4 - by, 4) * part, part)
        out_ref[pl.ds(at, part), :] = ref[...]


def join(blocks):
    part, width = blocks[0].shape
    return pl.pallas_call(
        join_kernel,
        out_shape=jax.ShapeDtypeStruct((4 * part, width), jnp.bfloat16),
        in_specs=[pl.BlockSpec(memory_space=pltpu.SMEM)] + [pl.BlockSpec(memory_space=pltpu.VMEM)] * 4,
        out_specs=pl.BlockSpec(memory_space=pltpu.VMEM),
        compiler_params=pltpu.CompilerParams(vmem_limit_bytes=16 * 1024 * 1024),
        cost_estimate=JOIN_COST,
        name="join",
    )(own_x().astype(jnp.int32).reshape(1), *blocks)


def body(
    acts,
    norm_gain,
    key_weight,
    key_cotangent,
    pending_delta,
    fragment_index,
    global_frag,
    outer_mom,
):
    weight = key_weight[0]
    go = fragment_index[0] >= 0
    far_weight = lax.ppermute(weight, "fsdp", ACROSS)

    half = (lax.axis_index("fsdp") // HALF).astype(jnp.int32).reshape(1)
    mixed = normalise(half, acts, norm_gain.reshape(D // LANES, LANES), key_cotangent)
    delta, mixed = lax.optimization_barrier((pending_delta[0], mixed))
    mixed = exchange(mixed.reshape(HALF * ROWS_IN, WIDE), "fsdp", HALVES)
    own = staged(go, reduce_x, delta)
    arrivals = [paired(own, bits) for bits in (6, 4, 2)]
    far_weight = hold(far_weight)
    mixed, far_weight = lax.optimization_barrier((mixed, far_weight))
    sent = far_gradient(mixed)
    arrived = lax.ppermute(sent, "fsdp", ACROSS)

    def second(mixed, own, arrivals, weight, far_weight):
        some = own.astype(jnp.float32)
        for part in arrivals:
            some += part.astype(jnp.float32)
        some = some.astype(jnp.bfloat16)
        blocks = [some] + [turned(some, by) for by in range(1, 4)]
        keys, stepped = near_work(mixed, weight, far_weight)
        return keys, stepped, blocks

    keys, stepped, blocks = staged(go, second, mixed, own, arrivals, weight, far_weight)
    ours = join(blocks)
    keys, ours = lax.optimization_barrier((keys, ours))
    theirs = paired(ours, 1)

    def third(keys):
        return sum_parts(exchange(keys, "fsdp", HALVES), HALF).astype(jnp.bfloat16)

    key_out = staged(go, third, keys)
    key_out, arrived, theirs = lax.optimization_barrier((key_out, arrived, theirs))
    new_weight, global_new, mom_new = blend(fragment_index, stepped, arrived, ours, theirs, global_frag, outer_mom)
    return (key_out, new_weight[None], global_new, mom_new)


def solution(mesh):
    in_specs = (
        P(("replica", "fsdp"), None),
        P(),
        P("replica", "fsdp", None),
        P(("replica", "fsdp"), None),
        P("replica", "fsdp", None),
        P(),
        P("fsdp", None),
        P("fsdp", None),
    )
    out_specs = (
        P(("replica", "fsdp"), None),
        P("replica", "fsdp", None),
        P("fsdp", None),
        P("fsdp", None),
    )
    return jax.shard_map(body, mesh=mesh, in_specs=in_specs, out_specs=out_specs, check_vma=False)
```
